256 devices in a mesh: dp: 256 (over y, z, x, core).
Axes of the slice: x: 4, y: 4, z: 8, core: 2. Of those that a mesh axis runs over, the one named last changes fastest.
Arguments:
- picture_vectors: bfloat16 [98304, 1152], P('dp'), may hold values from -6 to 6
- caption_vectors: bfloat16 [98304, 1152], P('dp'), may hold values from -6 to 6
- photo_couple_tags: int32 [98304], P('dp'), may hold values from 0 to 3071
- caption_match_ids: int32 [98304], P('dp'), may hold values from 0 to 3071
- affinity_stretch: float32 [1], replicated, may hold values from 2 to 4
- score_offset: float32 [1], replicated, may hold values from -3 to -1
Outputs:
- loss_rows: float32 [98304], P('dp')
- image_unit_gradient: float32 [98304, 1152], P('dp')
- text_unit_gradient: float32 [98304, 1152], P('dp')
The draws below stay inside these ranges and needn't reach their ends.
All inputs are finite; a program needn't handle non-finite values.
Results may differ from the reference program's by a relative error of at most 0.0039.
Values may be sent and summed in bfloat16 or wider, within the bound.
A program may use at most 64 MiB of HBM per device.

```python
import jax
import jax.numpy as jnp
from jax import lax

D = 1152
B_DEV = 384
REACH = 3
BATCH = 98304
N_DP = 256


def touch_ends(array, own_key, least, high):
    place = [jax.random.randint(jax.random.fold_in(own_key, axis), (), 0, length) for axis, length in enumerate(array.shape)]
    widest = array.shape.index(max(array.shape))
    neighbour = place[:widest] + [(place[widest] + 1) % array.shape[widest]] + place[widest + 1:]
    return array.at[tuple(place)].set(least).at[tuple(neighbour)].set(high)


def block_levels(own_key, extent, split, smallest, top_value):
    def one(axis_at, shards_of):
        draws = jax.random.uniform(jax.random.fold_in(jax.random.fold_in(own_key, 6), axis_at), (shards_of,), jnp.float32, smallest / len(split), top_value / len(split))
        return jnp.repeat(jnp.exp(draws), extent[axis_at] // shards_of).reshape((-1,) + (1,) * (len(extent) - axis_at - 1))

    loudness = one(*split[0])
    for cut in split[1:]:
        loudness = loudness * one(*cut)
    return loudness


def gaussian(own_key, dims, scale, most, cuts=(), kind=jnp.bfloat16):
    result = jax.random.normal(own_key, dims, jnp.float32) * scale
    if len(cuts) > 0:
        result = block_levels(own_key, dims, cuts, -0.22, 0.18) * result
    return jnp.clip(result, min=-most, max=most).astype(kind)


def setup_inputs(seed: int = 0) -> dict:
    seeds = jax.random.split(jax.random.key(seed), 7)
    picture_vectors = gaussian(seeds[0], (BATCH, D), 1.0, 6.0, ((0, 256),))
    caption_vectors = gaussian(seeds[1], (BATCH, D), 1.0, 6.0, ((0, 256),))
    photo_couple_tags = touch_ends(jax.random.randint(seeds[2], (BATCH,), 0, 8 * B_DEV), jax.random.fold_in(seeds[2], 1), 0, (8 * B_DEV) - 1).astype(jnp.int32)
    caption_match_ids = touch_ends(jax.random.randint(seeds[3], (BATCH,), 0, 8 * B_DEV), jax.random.fold_in(seeds[3], 1), 0, (8 * B_DEV) - 1).astype(jnp.int32)
    affinity_stretch = jnp.clip(jax.random.uniform(seeds[4], (1,), jnp.float32, 2.0, 4.0), 2.0, 4.0)
    score_offset = jnp.clip(jax.random.uniform(seeds[5], (1,), jnp.float32, -3.0, -1.0), -3.0, -1.0)
    return {"picture_vectors": picture_vectors, "caption_vectors": caption_vectors, "photo_couple_tags": photo_couple_tags, "caption_match_ids": caption_match_ids, "affinity_stretch": affinity_stretch, "score_offset": score_offset}


def unit_rows(value_entries):
    broadened = value_entries.astype(jnp.float32)
    reciprocal_warmth_gain = lax.rsqrt(lax.optimization_barrier(jnp.sum(broadened * broadened, axis=-1, keepdims=True)) + 1e-06)
    return (broadened * reciprocal_warmth_gain).astype(jnp.bfloat16)

def reference(picture_vectors, caption_vectors, photo_couple_tags, caption_match_ids, affinity_stretch, score_offset):
    batch_slices = N_DP
    img_blocks = unit_rows(picture_vectors).reshape(batch_slices, B_DEV, D)
    txt_blocks = unit_rows(caption_vectors).reshape(batch_slices, B_DEV, D)
    img_keys = photo_couple_tags.reshape(batch_slices, B_DEV)
    text_key_rows = caption_match_ids.reshape(batch_slices, B_DEV)
    reciprocal_warmth_gain = affinity_stretch[0]
    displacement = score_offset[0]

    def one_shard(txt_total, index):
        local_portion = lax.dynamic_index_in_dim(img_blocks, index, 0, keepdims=False)
        local_embedding_tiles = lax.dynamic_index_in_dim(img_keys, index, 0, keepdims=False)
        loss_sum = jnp.zeros((B_DEV,), jnp.float32)
        grad_sum = jnp.zeros((B_DEV, D), jnp.float32)
        for step in range(-REACH, REACH + 1):
            other = ((index + step) % batch_slices).astype(jnp.int32)
            visiting_portion = lax.dynamic_index_in_dim(txt_blocks, other, 0, keepdims=False)
            visiting_embedding_tiles = lax.dynamic_index_in_dim(text_key_rows, other, 0, keepdims=False)
            raw_affinity = reciprocal_warmth_gain * jnp.dot(local_portion, visiting_portion.T, preferred_element_type=jnp.float32) + displacement
            target_sign = jnp.where(local_embedding_tiles[:, None] == visiting_embedding_tiles[None, :], 1.0, -1.0).astype(jnp.float32)
            loss_sum = loss_sum + lax.optimization_barrier(jnp.sum(jax.nn.softplus(-target_sign * raw_affinity), axis=1))
            weighting_term = (-target_sign * jax.nn.sigmoid(-target_sign * raw_affinity) * reciprocal_warmth_gain).astype(jnp.bfloat16)
            grad_sum = grad_sum + jnp.dot(weighting_term, visiting_portion, preferred_element_type=jnp.float32)
            term = jnp.dot(weighting_term.T, local_portion, preferred_element_type=jnp.float32)
            current = lax.dynamic_index_in_dim(txt_total, other, 0, keepdims=False)
            txt_total = lax.dynamic_update_index_in_dim(txt_total, current + term, other, 0)
        return (txt_total, (loss_sum / ((2 * REACH + 1) * B_DEV), grad_sum))
    start = jnp.zeros((batch_slices, B_DEV, D), jnp.float32)
    txt_total, (loss_all, grad_all) = lax.scan(one_shard, start, jnp.arange(batch_slices, dtype=jnp.int32))
    return (loss_all.reshape(-1), grad_all.reshape(-1, D), txt_total.reshape(-1, D))
```

```python
import math

import jax
import jax.numpy as jnp
from jax import lax
from jax.experimental import pallas as pl
from jax.experimental.pallas import tpu as pltpu
from jax.sharding import PartitionSpec as P

MESH = pl.DeviceIdType.MESH
REACH = 3
ROWS = 128
OUT1, IN3, IN2, OUT2, IN1, OUT3 = range(6)
TEXT, IMAGE = 0, 1


def kernel(
    stretch_ref,
    offset_ref,
    picture_ref,
    caption_ref,
    couple_ref,
    match_ref,
    loss_ref,
    image_grad_ref,
    text_grad_ref,
    raw,
    own,
    held,
    own_tags,
    tags,
    columns,
    load_sem,
    send_sem,
    recv_sem,
    tag_send_sem,
    tag_recv_sem,
):
    count = lax.axis_size("dp")
    me = lax.axis_index("dp")
    sign = 2 * lax.rem(me, 2) - 1
    pieces = own.shape[1]

    def at(steps):
        return lax.rem(me + steps * sign + count, count)

    target = {OUT1: at(1), IN3: at(-3), IN2: at(-1), OUT2: at(-1), IN1: at(-1), OUT3: at(-2)}

    barrier = pltpu.get_barrier_semaphore()
    for steps in (1, -3, -1, 2):
        pl.semaphore_signal(barrier, inc=1, device_id=(at(steps),), device_id_type=MESH)

    def load(side, piece):
        source = (caption_ref, picture_ref)[side]
        return pltpu.make_async_copy(
            source.at[pl.ds(piece * ROWS, ROWS)], raw.at[side, piece], load_sem.at[side, piece]
        )

    for piece in range(pieces):
        for side in (TEXT, IMAGE):
            load(side, piece).start()

    half = 0.5 * stretch_ref[0]
    shift = 0.5 * offset_ref[0]

    def normalize(side, piece):
        load(side, piece).wait()
        value = raw[side, piece].astype(jnp.float32)
        gain = lax.rsqrt(jnp.sum(value * value, axis=-1, keepdims=True) + 1e-06)
        own[side, piece] = (value * gain).astype(jnp.bfloat16)

    def source_of(slot, side, piece):
        if slot in (OUT1, IN3, IN1):
            return own.at[side, piece]
        return held.at[side, piece, IN3 if slot == OUT2 else OUT1]

    def send(slot, side, piece):
        return pltpu.make_async_remote_copy(
            src_ref=source_of(slot, side, piece),
            dst_ref=held.at[side, piece, slot],
            send_sem=send_sem.at[slot, side, piece],
            recv_sem=recv_sem.at[slot, side, piece],
            device_id=(target[slot],),
            device_id_type=MESH,
        )

    def send_tags(slot):
        if slot in (OUT1, IN3, IN1):
            source = own_tags
        else:
            source = tags.at[IN3 if slot == OUT2 else OUT1]
        return pltpu.make_async_remote_copy(
            src_ref=source,
            dst_ref=tags.at[slot],
            send_sem=tag_send_sem.at[slot],
            recv_sem=tag_recv_sem.at[slot],
            device_id=(target[slot],),
            device_id_type=MESH,
        )

    own_tags[TEXT : TEXT + 1, :] = match_ref[...]
    own_tags[IMAGE : IMAGE + 1, :] = couple_ref[...]
    own_tags[2:8, :] = jnp.zeros((6, own_tags.shape[1]), jnp.int32)
    normalize(TEXT, 0)
    normalize(IMAGE, 0)
    pl.semaphore_wait(barrier, 4)
    for slot in (OUT1, IN3, IN1):
        send_tags(slot).start()
    for piece in range(pieces):
        if piece:
            normalize(TEXT, piece)
            normalize(IMAGE, piece)
        for side in (TEXT, IMAGE):
            for slot in (OUT1, IN3, IN1):
                send(slot, side, piece).start()

    for side, source in ((TEXT, couple_ref), (IMAGE, match_ref)):
        for piece in range(pieces):
            row = source[0:1, piece * ROWS : (piece + 1) * ROWS]
            columns[side, piece * ROWS : (piece + 1) * ROWS, :] = jnp.broadcast_to(
                row, (128, ROWS)
            ).T

    loss_ref[...] = jnp.zeros_like(loss_ref)

    def unit(side, block, row, first=False):
        mine = own[1 - side].reshape(-1, block.shape[1])
        total_ref = (image_grad_ref, text_grad_ref)[side]
        product = lax.dot_general(
            mine, block, (((1,), (1,)), ((), ())), preferred_element_type=jnp.float32
        )
        bend = jnp.tanh(half * product + shift)
        groups = block.shape[0] // 128
        equal = jnp.concatenate([columns[side]] * groups, axis=1) == row
        coef = (half * bend + jnp.where(equal, -half, half)).astype(jnp.bfloat16)
        if side == TEXT:
            kept = 1.0 - jnp.where(equal, -bend, bend)
            wide = kept[:, :128]
            for group in range(1, groups):
                wide = wide * kept[:, group * 128 : (group + 1) * 128]
            loss_ref[...] += jnp.log(wide)
        part = jnp.dot(coef, block, preferred_element_type=jnp.float32)
        if first:
            total_ref[...] = part
        else:
            total_ref[...] += part

    def slot_tags(side, piece, slots):
        span = pl.ds(pl.multiple_of(piece * ROWS, ROWS), ROWS)
        return jnp.concatenate([tags[slot, side : side + 1, span] for slot in slots], axis=1)

    def slot_unit(side, piece, low, high):
        block = held[side, piece, low : high + 1].reshape(-1, held.shape[-1])
        unit(side, block, slot_tags(side, piece, range(low, high + 1)))

    for side in (TEXT, IMAGE):
        block = own[side].reshape(-1, own.shape[-1])
        unit(side, block, own_tags[side : side + 1, :], first=True)

    send_tags(IN1).wait_recv()
    for side in (TEXT, IMAGE):

        def near_body(piece, carry, side=side):
            send(IN1, side, piece).wait_recv()
            slot_unit(side, piece, IN1, IN1)
            return carry

        lax.fori_loop(0, pieces, near_body, 0)

    send_tags(OUT1).wait_recv()
    send_tags(IN2).start()
    send_tags(OUT3).start()
    send_tags(IN3).wait_recv()
    send_tags(OUT2).start()
    send_tags(IN2).wait_recv()
    send_tags(OUT2).wait_recv()
    send_tags(OUT3).wait_recv()

    def body(piece, carry):
        for side in (TEXT, IMAGE):
            send(OUT1, side, piece).wait_recv()
            send(IN2, side, piece).start()
            send(OUT3, side, piece).start()
            send(IN3, side, piece).wait_recv()
            send(OUT2, side, piece).start()
        for side in (TEXT, IMAGE):
            slot_unit(side, piece, OUT1, IN3)
        for side in (TEXT, IMAGE):
            send(IN2, side, piece).wait_recv()
            send(OUT2, side, piece).wait_recv()
            slot_unit(side, piece, IN2, OUT2)
        return carry

    lax.fori_loop(0, pieces, body, 0)

    def last_body(piece, carry):
        for side in (TEXT, IMAGE):
            send(OUT3, side, piece).wait_recv()
            slot_unit(side, piece, OUT3, OUT3)
        return carry

    lax.fori_loop(0, pieces, last_body, 0)

    for slot in range(6):
        send_tags(slot).wait_send()

        def drain(piece, carry, slot=slot):
            for side in (TEXT, IMAGE):
                send(slot, side, piece).wait_send()
            return carry

        lax.fori_loop(0, pieces, drain, 0)


def shards(
    picture_vectors,
    caption_vectors,
    photo_couple_tags,
    caption_match_ids,
    affinity_stretch,
    score_offset,
):
    rows, width = picture_vectors.shape
    pieces = rows // ROWS
    vmem = pl.BlockSpec(memory_space=pltpu.VMEM)
    smem = pl.BlockSpec(memory_space=pltpu.SMEM)
    anywhere = pl.BlockSpec(memory_space=pl.ANY)
    loss_parts, image_unit_gradient, text_unit_gradient = pl.pallas_call(
        kernel,
        out_shape=(
            jax.ShapeDtypeStruct((rows, 128), jnp.float32),
            jax.ShapeDtypeStruct((rows, width), jnp.float32),
            jax.ShapeDtypeStruct((rows, width), jnp.float32),
        ),
        in_specs=[smem, smem, anywhere, anywhere, vmem, vmem],
        out_specs=(vmem, vmem, vmem),
        scratch_shapes=[
            pltpu.VMEM((2, pieces, ROWS, width), jnp.bfloat16),
            pltpu.VMEM((2, pieces, ROWS, width), jnp.bfloat16),
            pltpu.VMEM((2, pieces, 6, ROWS, width), jnp.bfloat16),
            pltpu.VMEM((8, rows), jnp.int32),
            pltpu.VMEM((6, 8, rows), jnp.int32),
            pltpu.VMEM((2, rows, 128), jnp.int32),
            pltpu.SemaphoreType.DMA((2, pieces)),
            pltpu.SemaphoreType.DMA((6, 2, pieces)),
            pltpu.SemaphoreType.DMA((6, 2, pieces)),
            pltpu.SemaphoreType.DMA((6,)),
            pltpu.SemaphoreType.DMA((6,)),
        ],
        compiler_params=pltpu.CompilerParams(
            collective_id=0, has_side_effects=True, vmem_limit_bytes=40 * 1024 * 1024
        ),
        name="window_loss",
    )(
        affinity_stretch,
        score_offset,
        picture_vectors,
        caption_vectors,
        photo_couple_tags.reshape(1, rows),
        caption_match_ids.reshape(1, rows),
    )
    loss_rows = math.log(2.0) - jnp.sum(loss_parts, axis=1) / ((2 * REACH + 1) * rows)
    return (loss_rows, image_unit_gradient, text_unit_gradient)


def solution(mesh):
    placed = (P("dp", None), P("dp", None), P("dp"), P("dp"), P(), P())
    return jax.shard_map(
        shards,
        mesh=mesh,
        in_specs=placed,
        out_specs=(P("dp"), P("dp", None), P("dp", None)),
        check_vma=False,
    )
```

```python
import math

import jax
import jax.numpy as jnp
from jax import lax
from jax.experimental import pallas as pl
from jax.experimental.pallas import tpu as pltpu
from jax.sharding import PartitionSpec as P

MESH = pl.DeviceIdType.MESH
REACH = 3
ROWS = 128
OUT1, IN3, IN2, OUT2, IN1, OUT3 = range(6)
TEXT, IMAGE = 0, 1


def kernel(
    stretch_hbm,
    offset_hbm,
    picture_ref,
    caption_ref,
    couple_ref,
    match_ref,
    loss_ref,
    image_grad_ref,
    text_grad_ref,
    raw,
    own,
    held,
    stretch_ref,
    offset_ref,
    flat_tags,
    own_tags,
    tags,
    columns,
    load_sem,
    tag_load_sem,
    send_sem,
    recv_sem,
    tag_send_sem,
    tag_recv_sem,
):
    count = lax.axis_size("dp")
    me = lax.axis_index("dp")
    sign = 2 * lax.rem(me, 2) - 1
    pieces = own.shape[1]

    def at(steps):
        return lax.rem(me + steps * sign + count, count)

    target = {OUT1: at(1), IN3: at(-3), IN2: at(-1), OUT2: at(-1), IN1: at(-1), OUT3: at(-2)}

    barrier = pltpu.get_barrier_semaphore()
    for steps in (1, -3, -1, 2):
        pl.semaphore_signal(barrier, inc=1, device_id=(at(steps),), device_id_type=MESH)

    def load(side, piece):
        source = (caption_ref, picture_ref)[side]
        return pltpu.make_async_copy(
            source.at[pl.ds(piece * ROWS, ROWS)], raw.at[side, piece], load_sem.at[side, piece]
        )

    def load_tags(side):
        source = (match_ref, couple_ref)[side]
        return pltpu.make_async_copy(source, flat_tags[side], tag_load_sem.at[side])

    for piece in range(pieces):
        for side in (TEXT, IMAGE):
            load(side, piece).start()
            if piece == 0:
                load_tags(side).start()

    scalars = (
        pltpu.make_async_copy(stretch_hbm, stretch_ref, tag_load_sem.at[2]),
        pltpu.make_async_copy(offset_hbm, offset_ref, tag_load_sem.at[3]),
    )
    for copy in scalars:
        copy.start()

    def normalize(side, piece):
        load(side, piece).wait()
        value = raw[side, piece].astype(jnp.float32)
        gain = lax.rsqrt(jnp.sum(value * value, axis=-1, keepdims=True) + 1e-06)
        own[side, piece] = (value * gain).astype(jnp.bfloat16)

    def source_of(slot, side, piece):
        if slot in (OUT1, IN3, IN1):
            return own.at[side, piece]
        return held.at[side, piece, IN3 if slot == OUT2 else OUT1]

    def send(slot, side, piece):
        return pltpu.make_async_remote_copy(
            src_ref=source_of(slot, side, piece),
            dst_ref=held.at[side, piece, slot],
            send_sem=send_sem.at[slot, side, piece],
            recv_sem=recv_sem.at[slot, side, piece],
            device_id=(target[slot],),
            device_id_type=MESH,
        )

    def send_tags(slot):
        if slot in (OUT1, IN3, IN1):
            source = own_tags
        else:
            source = tags.at[IN3 if slot == OUT2 else OUT1]
        return pltpu.make_async_remote_copy(
            src_ref=source,
            dst_ref=tags.at[slot],
            send_sem=tag_send_sem.at[slot],
            recv_sem=tag_recv_sem.at[slot],
            device_id=(target[slot],),
            device_id_type=MESH,
        )

    rows = own_tags.shape[1]
    for side in (TEXT, IMAGE):
        load_tags(side).wait()
        own_tags[side : side + 1, :] = flat_tags[side][...].reshape(1, rows)
    own_tags[2:8, :] = jnp.zeros((6, own_tags.shape[1]), jnp.int32)
    normalize(TEXT, 0)
    normalize(IMAGE, 0)
    pl.semaphore_wait(barrier, 4)
    for slot in (OUT1, IN3, IN1):
        send_tags(slot).start()
    for piece in range(pieces):
        if piece:
            normalize(TEXT, piece)
            normalize(IMAGE, piece)
        for side in (TEXT, IMAGE):
            send(OUT1, side, piece).start()
            if piece == 0:
                send(IN3, side, piece).start()
            send(IN1, side, piece).start()

    for side in (TEXT, IMAGE):
        for piece in range(pieces):
            row = own_tags[1 - side : 2 - side, piece * ROWS : (piece + 1) * ROWS]
            columns[side, piece * ROWS : (piece + 1) * ROWS, :] = jnp.broadcast_to(
                row, (128, ROWS)
            ).T

    for copy in scalars:
        copy.wait()
    half = 0.5 * stretch_ref[0]
    shift = 0.5 * offset_ref[0]
    loss_ref[...] = jnp.zeros_like(loss_ref)

    def unit(side, block, row, first=False):
        mine = own[1 - side].reshape(-1, block.shape[1])
        total_ref = (image_grad_ref, text_grad_ref)[side]
        product = lax.dot_general(
            mine, block, (((1,), (1,)), ((), ())), preferred_element_type=jnp.float32
        )
        bend = jnp.tanh(half * product + shift)
        groups = block.shape[0] // 128
        equal = jnp.concatenate([columns[side]] * groups, axis=1) == row
        coef = (half * bend + jnp.where(equal, -half, half)).astype(jnp.bfloat16)
        if side == TEXT:
            kept = 1.0 - jnp.where(equal, -bend, bend)
            wide = kept[:, :128]
            for group in range(1, groups):
                wide = wide * kept[:, group * 128 : (group + 1) * 128]
            loss_ref[...] += jnp.log(wide)
        part = jnp.dot(coef, block, preferred_element_type=jnp.float32)
        if first:
            total_ref[...] = part
        else:
            total_ref[...] += part

    def slot_tags(side, piece, slots):
        span = pl.ds(pl.multiple_of(piece * ROWS, ROWS), ROWS)
        return jnp.concatenate([tags[slot, side : side + 1, span] for slot in slots], axis=1)

    def slot_unit(side, piece, low, high):
        block = held[side, piece, low : high + 1].reshape(-1, held.shape[-1])
        unit(side, block, slot_tags(side, piece, range(low, high + 1)))

    for side in (TEXT, IMAGE):
        block = own[side].reshape(-1, own.shape[-1])
        unit(side, block, own_tags[side : side + 1, :], first=True)

    send_tags(IN1).wait_recv()

    def near_body(piece, carry):
        for side in (TEXT, IMAGE):
            send(IN1, side, piece).wait_recv()
        for side in (TEXT, IMAGE):
            slot_unit(side, piece, IN1, IN1)
        return carry

    lax.fori_loop(0, pieces, near_body, 0)

    send_tags(OUT1).wait_recv()
    send_tags(IN2).start()
    send_tags(OUT3).start()
    send_tags(IN3).wait_recv()
    send_tags(OUT2).start()
    send_tags(IN2).wait_recv()
    send_tags(OUT2).wait_recv()
    send_tags(OUT3).wait_recv()

    def last_piece(piece):
        for side in (TEXT, IMAGE):
            send(OUT3, side, piece).wait_recv()
        for side in (TEXT, IMAGE):
            slot_unit(side, piece, OUT3, OUT3)

    def body(piece, carry):
        for side in (TEXT, IMAGE):
            send(OUT1, side, piece).wait_recv()
            send(IN2, side, piece).start()
            send(OUT3, side, piece).start()

            @pl.when(piece + 1 < pieces)
            def _(side=side):
                send(IN3, side, piece + 1).start()

            send(IN3, side, piece).wait_recv()
            send(OUT2, side, piece).start()
        for side in (TEXT, IMAGE):
            slot_unit(side, piece, OUT1, IN3)
        for side in (TEXT, IMAGE):
            send(IN2, side, piece).wait_recv()
            send(OUT2, side, piece).wait_recv()
        for side in (TEXT, IMAGE):
            slot_unit(side, piece, IN2, OUT2)

        @pl.when(piece > 0)
        def _():
            last_piece(piece - 1)

        return carry

    lax.fori_loop(0, pieces, body, 0)

    last_piece(pieces - 1)

    for slot in range(6):
        send_tags(slot).wait_send()

        def drain(piece, carry, slot=slot):
            for side in (TEXT, IMAGE):
                send(slot, side, piece).wait_send()
            return carry

        lax.fori_loop(0, pieces, drain, 0)


def finish(loss_ref, image_grad_ref, text_grad_ref, loss_out, image_out, text_out, sem):
    rows, lanes = loss_ref.shape
    copies = []
    for piece in range(rows // ROWS):
        span = pl.ds(piece * ROWS, ROWS)
        for side, (source, target) in enumerate(
            ((text_grad_ref, text_out), (image_grad_ref, image_out))
        ):
            copies.append(
                pltpu.make_async_copy(source.at[span], target.at[span], sem.at[side, piece])
            )
    for copy in copies:
        copy.start()
    sums = lax.dot_general(
        jnp.ones((8, lanes), jnp.float32),
        loss_ref[...],
        (((1,), (1,)), ((), ())),
        precision=lax.Precision.HIGHEST,
        preferred_element_type=jnp.float32,
    )
    loss = math.log(2.0) - sums[0:1] / ((2 * REACH + 1) * rows)
    loss_out[...] = loss.reshape(rows)
    for copy in copies:
        copy.wait()


def shards(
    picture_vectors,
    caption_vectors,
    photo_couple_tags,
    caption_match_ids,
    affinity_stretch,
    score_offset,
):
    rows, width = picture_vectors.shape
    pieces = rows // ROWS
    operands = (
        affinity_stretch,
        score_offset,
        picture_vectors,
        caption_vectors,
        photo_couple_tags,
        caption_match_ids,
    )
    vmem = pl.BlockSpec(memory_space=pltpu.VMEM)
    hbm = pl.BlockSpec(memory_space=pltpu.HBM)
    loss_parts, image_unit_gradient, text_unit_gradient = pl.pallas_call(
        kernel,
        out_shape=(
            pltpu.VMEM((rows, 128), jnp.float32),
            pltpu.VMEM((rows, width), jnp.float32),
            pltpu.VMEM((rows, width), jnp.float32),
        ),
        in_specs=[hbm] * 6,
        out_specs=(vmem, vmem, vmem),
        scratch_shapes=[
            pltpu.VMEM((2, pieces, ROWS, width), jnp.bfloat16),
            pltpu.VMEM((2, pieces, ROWS, width), jnp.bfloat16),
            pltpu.VMEM((2, pieces, 6, ROWS, width), jnp.bfloat16),
            pltpu.SMEM((1,), jnp.float32),
            pltpu.SMEM((1,), jnp.float32),
            [pltpu.VMEM((rows,), jnp.int32)] * 2,
            pltpu.VMEM((8, rows), jnp.int32),
            pltpu.VMEM((6, 8, rows), jnp.int32),
            pltpu.VMEM((2, rows, 128), jnp.int32),
            pltpu.SemaphoreType.DMA((2, pieces)),
            pltpu.SemaphoreType.DMA((4,)),
            pltpu.SemaphoreType.DMA((6, 2, pieces)),
            pltpu.SemaphoreType.DMA((6, 2, pieces)),
            pltpu.SemaphoreType.DMA((6,)),
            pltpu.SemaphoreType.DMA((6,)),
        ],
        compiler_params=pltpu.CompilerParams(
            collective_id=0, has_side_effects=True, vmem_limit_bytes=40 * 1024 * 1024
        ),
        name="window_loss",
    )(
        *(
            pltpu.with_memory_space_constraint(array, pltpu.HBM) if array.size > 1 else array
            for array in operands
        )
    )
    return pl.pallas_call(
        finish,
        out_shape=(
            jax.ShapeDtypeStruct((rows,), jnp.float32),
            jax.ShapeDtypeStruct((rows, width), jnp.float32),
            jax.ShapeDtypeStruct((rows, width), jnp.float32),
        ),
        in_specs=[vmem, vmem, vmem],
        out_specs=(vmem, hbm, hbm),
        scratch_shapes=[pltpu.SemaphoreType.DMA((2, pieces))],
        compiler_params=pltpu.CompilerParams(vmem_limit_bytes=8 * 1024 * 1024),
        name="write_out",
    )(loss_parts, image_unit_gradient, text_unit_gradient)


def solution(mesh):
    placed = (P("dp", None), P("dp", None), P("dp"), P("dp"), P(), P())
    return jax.shard_map(
        shards,
        mesh=mesh,
        in_specs=placed,
        out_specs=(P("dp"), P("dp", None), P("dp", None)),
        check_vma=False,
    )
```

```python
import math

import jax
import jax.numpy as jnp
from jax import lax
from jax.experimental import pallas as pl
from jax.experimental.pallas import tpu as pltpu
from jax.sharding import PartitionSpec as P

MESH = pl.DeviceIdType.MESH
REACH = 3
ROWS = 128
LEAD = 2
OUT1, IN3, IN2, OUT2, IN1, OUT3 = range(6)
TEXT, IMAGE = 0, 1


def kernel(
    stretch_hbm,
    offset_hbm,
    picture_ref,
    caption_ref,
    couple_ref,
    match_ref,
    loss_ref,
    image_grad_ref,
    text_grad_ref,
    coef_ref,
    block_ref,
    raw,
    own,
    held,
    stretch_ref,
    offset_ref,
    flat_tags,
    own_tags,
    tags,
    columns,
    load_sem,
    tag_load_sem,
    send_sem,
    recv_sem,
    tag_send_sem,
    tag_recv_sem,
):
    count = lax.axis_size("dp")
    me = lax.axis_index("dp")
    sign = 2 * lax.rem(me, 2) - 1
    pieces = own.shape[1]

    def at(steps):
        return lax.rem(me + steps * sign + count, count)

    target = {OUT1: at(1), IN3: at(-3), IN2: at(-1), OUT2: at(-1), IN1: at(-1), OUT3: at(-2)}

    barrier = pltpu.get_barrier_semaphore()
    for steps in (1, -3, -1, 2):
        pl.semaphore_signal(barrier, inc=1, device_id=(at(steps),), device_id_type=MESH)

    def load(side, piece):
        source = (caption_ref, picture_ref)[side]
        return pltpu.make_async_copy(
            source.at[pl.ds(piece * ROWS, ROWS)], raw.at[side, piece], load_sem.at[side, piece]
        )

    def load_tags(side):
        source = (match_ref, couple_ref)[side]
        return pltpu.make_async_copy(source, flat_tags[side], tag_load_sem.at[side])

    for side in (TEXT, IMAGE):
        load_tags(side).start()
    for side in (TEXT, IMAGE):
        for piece in range(pieces):
            load(side, piece).start()
    scalars = (
        pltpu.make_async_copy(stretch_hbm, stretch_ref, tag_load_sem.at[2]),
        pltpu.make_async_copy(offset_hbm, offset_ref, tag_load_sem.at[3]),
    )
    for copy in scalars:
        copy.start()

    def normalize(side, piece):
        load(side, piece).wait()
        value = raw[side, piece].astype(jnp.float32)
        gain = lax.rsqrt(jnp.sum(value * value, axis=-1, keepdims=True) + 1e-06)
        own[side, piece] = (value * gain).astype(jnp.bfloat16)

    def source_of(slot, side, piece):
        if slot in (OUT1, IN3, IN1):
            return own.at[side, piece]
        return held.at[side, piece, IN3 if slot == OUT2 else OUT1]

    def send(slot, side, piece):
        return pltpu.make_async_remote_copy(
            src_ref=source_of(slot, side, piece),
            dst_ref=held.at[side, piece, slot],
            send_sem=send_sem.at[slot, side, piece],
            recv_sem=recv_sem.at[slot, side, piece],
            device_id=(target[slot],),
            device_id_type=MESH,
        )

    def send_tags(slot):
        if slot in (OUT1, IN3, IN1):
            source = own_tags
        else:
            source = tags.at[IN3 if slot == OUT2 else OUT1]
        return pltpu.make_async_remote_copy(
            src_ref=source,
            dst_ref=tags.at[slot],
            send_sem=tag_send_sem.at[slot],
            recv_sem=tag_recv_sem.at[slot],
            device_id=(target[slot],),
            device_id_type=MESH,
        )

    rows = own_tags.shape[1]
    for side in (TEXT, IMAGE):
        load_tags(side).wait()
        own_tags[side : side + 1, :] = flat_tags[side][...].reshape(1, rows)
    own_tags[2:8, :] = jnp.zeros((6, own_tags.shape[1]), jnp.int32)
    normalize(TEXT, 0)
    pl.semaphore_wait(barrier, 4)
    for slot in (OUT1, IN3, IN1):
        send_tags(slot).start()
    for side in (TEXT, IMAGE):
        for piece in range(pieces):
            if piece or side:
                normalize(side, piece)
            send(OUT1, side, piece).start()
            if side == TEXT and piece < LEAD:
                send(IN3, side, piece).start()
            send(IN1, side, piece).start()

    for side in (TEXT, IMAGE):
        for piece in range(pieces):
            row = own_tags[1 - side : 2 - side, piece * ROWS : (piece + 1) * ROWS]
            columns[side, piece * ROWS : (piece + 1) * ROWS, :] = jnp.broadcast_to(
                row, (128, ROWS)
            ).T

    for copy in scalars:
        copy.wait()
    half = 0.5 * stretch_ref[0]
    shift = 0.5 * offset_ref[0]
    loss_ref[...] = jnp.zeros_like(loss_ref)

    def weigh(side, block, row):
        mine = own[1 - side].reshape(-1, block.shape[1])
        product = lax.dot_general(
            mine, block, (((1,), (1,)), ((), ())), preferred_element_type=jnp.float32
        )
        bend = jnp.tanh(half * product + shift)
        equal = jnp.concatenate([columns[side]] * (block.shape[0] // 128), axis=1) == row
        coef = half * bend + jnp.where(equal, -half, half)
        return coef.astype(jnp.bfloat16), 1.0 - jnp.where(equal, -bend, bend)

    def unit(side, block, row, first=False):
        total_ref = (image_grad_ref, text_grad_ref)[side]
        coef, kept = weigh(side, block, row)
        if side == TEXT:
            wide = kept[:, :128]
            for group in range(1, block.shape[0] // 128):
                wide = wide * kept[:, group * 128 : (group + 1) * 128]
            loss_ref[...] += jnp.log(wide)
        part = jnp.dot(coef, block, preferred_element_type=jnp.float32)
        if first:
            total_ref[...] = part
        else:
            total_ref[...] += part

    def slot_tags(side, piece, slots):
        span = pl.ds(pl.multiple_of(piece * ROWS, ROWS), ROWS)
        return jnp.concatenate([tags[slot, side : side + 1, span] for slot in slots], axis=1)

    def slot_unit(side, piece, low, high):
        block = held[side, piece, low : high + 1].reshape(-1, held.shape[-1])
        unit(side, block, slot_tags(side, piece, range(low, high + 1)))

    for side in (TEXT, IMAGE):
        block = own[side].reshape(-1, own.shape[-1])
        unit(side, block, own_tags[side : side + 1, :], first=True)

    send_tags(IN1).wait_recv()

    def near_body(piece, carry):
        for side in (TEXT, IMAGE):
            send(IN1, side, piece).wait_recv()
        for side in (TEXT, IMAGE):
            slot_unit(side, piece, IN1, IN1)
        return carry

    lax.fori_loop(0, pieces, near_body, 0)

    send_tags(OUT1).wait_recv()
    send_tags(IN2).start()
    send_tags(OUT3).start()
    send_tags(IN3).wait_recv()
    send_tags(OUT2).start()
    send_tags(IN2).wait_recv()
    send_tags(OUT2).wait_recv()
    send_tags(OUT3).wait_recv()

    def relayed(side, piece):
        send(OUT3, side, piece).wait_recv()
        slot_unit(side, piece, OUT3, OUT3)

    for side in (TEXT, IMAGE):

        def body(piece, carry, side=side):
            send(OUT1, side, piece).wait_recv()
            send(IN2, side, piece).start()
            send(OUT3, side, piece).start()

            @pl.when(piece + LEAD < pieces)
            def _():
                send(IN3, side, piece + LEAD).start()

            if side == TEXT:

                @pl.when(piece + LEAD >= pieces)
                def _():
                    send(IN3, IMAGE, piece + LEAD - pieces).start()

            send(IN3, side, piece).wait_recv()
            send(OUT2, side, piece).start()
            slot_unit(side, piece, OUT1, IN3)
            send(IN2, side, piece).wait_recv()
            send(OUT2, side, piece).wait_recv()
            slot_unit(side, piece, IN2, OUT2)

            @pl.when(piece > 0)
            def _():
                relayed(side, piece - 1)

            if side == IMAGE:

                @pl.when(piece == 0)
                def _():
                    relayed(TEXT, pieces - 1)

            return carry

        lax.fori_loop(0, pieces, body, 0)

    send(OUT3, IMAGE, pieces - 1).wait_recv()
    block = held[IMAGE, pieces - 1, OUT3]
    coef_ref[...] = weigh(IMAGE, block, slot_tags(IMAGE, pieces - 1, [OUT3]))[0]
    block_ref[...] = block

    for slot in range(6):
        send_tags(slot).wait_send()

        def drain(piece, carry, slot=slot):
            for side in (TEXT, IMAGE):
                send(slot, side, piece).wait_send()
            return carry

        lax.fori_loop(0, pieces, drain, 0)


def finish(
    loss_ref, image_grad_ref, text_grad_ref, coef_ref, block_ref, loss_out, image_out, text_out, total, sem
):
    rows, lanes = loss_ref.shape
    copies = []

    def write(side, piece):
        span = pl.ds(piece * ROWS, ROWS)
        source, target = ((total, text_out), (image_grad_ref, image_out))[side]
        copy = pltpu.make_async_copy(source.at[span], target.at[span], sem.at[side, piece])
        copy.start()
        copies.append(copy)

    for piece in range(rows // ROWS):
        write(IMAGE, piece)
    for piece in range(rows // ROWS):
        span = pl.ds(piece * ROWS, ROWS)
        total[span] = text_grad_ref[span] + jnp.dot(
            coef_ref[span], block_ref[...], preferred_element_type=jnp.float32
        )
        write(TEXT, piece)
    sums = lax.dot_general(
        jnp.ones((8, lanes), jnp.float32),
        loss_ref[...],
        (((1,), (1,)), ((), ())),
        precision=lax.Precision.HIGHEST,
        preferred_element_type=jnp.float32,
    )
    loss = math.log(2.0) - sums[0:1] / ((2 * REACH + 1) * rows)
    loss_out[...] = loss.reshape(rows)
    for copy in copies:
        copy.wait()


def shards(
    picture_vectors,
    caption_vectors,
    photo_couple_tags,
    caption_match_ids,
    affinity_stretch,
    score_offset,
):
    rows, width = picture_vectors.shape
    pieces = rows // ROWS
    operands = (
        affinity_stretch,
        score_offset,
        picture_vectors,
        caption_vectors,
        photo_couple_tags,
        caption_match_ids,
    )
    vmem = pl.BlockSpec(memory_space=pltpu.VMEM)
    hbm = pl.BlockSpec(memory_space=pltpu.HBM)
    parts = pl.pallas_call(
        kernel,
        out_shape=(
            pltpu.VMEM((rows, 128), jnp.float32),
            pltpu.VMEM((rows, width), jnp.float32),
            pltpu.VMEM((rows, width), jnp.float32),
            pltpu.VMEM((rows, ROWS), jnp.bfloat16),
            pltpu.VMEM((ROWS, width), jnp.bfloat16),
        ),
        in_specs=[hbm] * 6,
        out_specs=(vmem,) * 5,
        scratch_shapes=[
            pltpu.VMEM((2, pieces, ROWS, width), jnp.bfloat16),
            pltpu.VMEM((2, pieces, ROWS, width), jnp.bfloat16),
            pltpu.VMEM((2, pieces, 6, ROWS, width), jnp.bfloat16),
            pltpu.SMEM((1,), jnp.float32),
            pltpu.SMEM((1,), jnp.float32),
            [pltpu.VMEM((rows,), jnp.int32)] * 2,
            pltpu.VMEM((8, rows), jnp.int32),
            pltpu.VMEM((6, 8, rows), jnp.int32),
            pltpu.VMEM((2, rows, 128), jnp.int32),
            pltpu.SemaphoreType.DMA((2, pieces)),
            pltpu.SemaphoreType.DMA((4,)),
            pltpu.SemaphoreType.DMA((6, 2, pieces)),
            pltpu.SemaphoreType.DMA((6, 2, pieces)),
            pltpu.SemaphoreType.DMA((6,)),
            pltpu.SemaphoreType.DMA((6,)),
        ],
        compiler_params=pltpu.CompilerParams(
            collective_id=0, has_side_effects=True, vmem_limit_bytes=40 * 1024 * 1024
        ),
        name="window_loss",
    )(
        *(
            pltpu.with_memory_space_constraint(array, pltpu.HBM) if array.size > 1 else array
            for array in operands
        )
    )
    return pl.pallas_call(
        finish,
        out_shape=(
            jax.ShapeDtypeStruct((rows,), jnp.float32),
            jax.ShapeDtypeStruct((rows, width), jnp.float32),
            jax.ShapeDtypeStruct((rows, width), jnp.float32),
        ),
        in_specs=[vmem] * 5,
        out_specs=(vmem, hbm, hbm),
        scratch_shapes=[pltpu.VMEM((rows, width), jnp.float32), pltpu.SemaphoreType.DMA((2, pieces))],
        compiler_params=pltpu.CompilerParams(vmem_limit_bytes=8 * 1024 * 1024),
        name="write_out",
    )(*parts)


def solution(mesh):
    placed = (P("dp", None), P("dp", None), P("dp"), P("dp"), P(), P())
    return jax.shard_map(
        shards,
        mesh=mesh,
        in_specs=placed,
        out_specs=(P("dp"), P("dp", None), P("dp", None)),
        check_vma=False,
    )
```

```python
import math

import jax
import jax.numpy as jnp
from jax import lax
from jax.experimental import pallas as pl
from jax.experimental.pallas import tpu as pltpu
from jax.sharding import PartitionSpec as P

MESH = pl.DeviceIdType.MESH
REACH = 3
ROWS = 128
LEAD = 2
OUT1, IN3, IN2, OUT2, IN1, OUT3 = range(6)
TEXT, IMAGE = 0, 1


def kernel(
    stretch_hbm,
    offset_hbm,
    picture_ref,
    caption_ref,
    couple_ref,
    match_ref,
    loss_ref,
    image_grad_ref,
    text_grad_ref,
    coef_ref,
    block_ref,
    raw,
    own,
    held,
    stretch_ref,
    offset_ref,
    flat_tags,
    own_tags,
    tags,
    columns,
    load_sem,
    tag_load_sem,
    send_sem,
    recv_sem,
    tag_send_sem,
    tag_recv_sem,
):
    count = lax.axis_size("dp")
    me = lax.axis_index("dp")
    sign = 2 * lax.rem(me, 2) - 1
    pieces = own.shape[1]

    def at(steps):
        return lax.rem(me + steps * sign + count, count)

    target = {OUT1: at(1), IN3: at(-3), IN2: at(-1), OUT2: at(-1), IN1: at(-1), OUT3: at(-2)}

    barrier = pltpu.get_barrier_semaphore()
    for steps in (1, -3, -1, 2):
        pl.semaphore_signal(barrier, inc=1, device_id=(at(steps),), device_id_type=MESH)

    def load(side, piece):
        source = (caption_ref, picture_ref)[side]
        return pltpu.make_async_copy(
            source.at[pl.ds(piece * ROWS, ROWS)], raw.at[side, piece], load_sem.at[side, piece]
        )

    def load_tags(side):
        source = (match_ref, couple_ref)[side]
        return pltpu.make_async_copy(source, flat_tags[side], tag_load_sem.at[side])

    for side in (TEXT, IMAGE):
        load_tags(side).start()
    for side in (TEXT, IMAGE):
        for piece in range(pieces):
            load(side, piece).start()
    scalars = (
        pltpu.make_async_copy(stretch_hbm, stretch_ref, tag_load_sem.at[2]),
        pltpu.make_async_copy(offset_hbm, offset_ref, tag_load_sem.at[3]),
    )
    for copy in scalars:
        copy.start()

    def normalize(side, piece):
        load(side, piece).wait()
        value = raw[side, piece].astype(jnp.float32)
        gain = lax.rsqrt(jnp.sum(value * value, axis=-1, keepdims=True) + 1e-06)
        own[side, piece] = (value * gain).astype(jnp.bfloat16)

    def source_of(slot, side, piece):
        if slot in (OUT1, IN3, IN1):
            return own.at[side, piece]
        return held.at[side, piece, IN3 if slot == OUT2 else OUT1]

    def send(slot, side, piece):
        return pltpu.make_async_remote_copy(
            src_ref=source_of(slot, side, piece),
            dst_ref=held.at[side, piece, slot],
            send_sem=send_sem.at[slot, side, piece],
            recv_sem=recv_sem.at[slot, side, piece],
            device_id=(target[slot],),
            device_id_type=MESH,
        )

    def send_tags(slot):
        if slot in (OUT1, IN3, IN1):
            source = own_tags
        else:
            source = tags.at[IN3 if slot == OUT2 else OUT1]
        return pltpu.make_async_remote_copy(
            src_ref=source,
            dst_ref=tags.at[slot],
            send_sem=tag_send_sem.at[slot],
            recv_sem=tag_recv_sem.at[slot],
            device_id=(target[slot],),
            device_id_type=MESH,
        )

    rows = own_tags.shape[1]
    for side in (TEXT, IMAGE):
        load_tags(side).wait()
        own_tags[side : side + 1, :] = flat_tags[side][...].reshape(1, rows)
    own_tags[2:8, :] = jnp.zeros((6, own_tags.shape[1]), jnp.int32)
    normalize(TEXT, 0)
    pl.semaphore_wait(barrier, 4)
    for slot in (OUT1, IN3, IN1):
        send_tags(slot).start()
    for side in (TEXT, IMAGE):
        for piece in range(pieces):
            if piece or side:
                normalize(side, piece)
            send(OUT1, side, piece).start()
            if side == TEXT and piece < LEAD:
                send(IN3, side, piece).start()
            send(IN1, side, piece).start()

    for side in (TEXT, IMAGE):
        for piece in range(pieces):
            row = own_tags[1 - side : 2 - side, piece * ROWS : (piece + 1) * ROWS]
            columns[side, piece * ROWS : (piece + 1) * ROWS, :] = jnp.broadcast_to(
                row, (128, ROWS)
            ).T

    for copy in scalars:
        copy.wait()
    half = 0.5 * stretch_ref[0]
    shift = 0.5 * offset_ref[0]
    loss_ref[...] = jnp.zeros_like(loss_ref)

    def weigh(side, block, row):
        mine = own[1 - side].reshape(-1, block.shape[1])
        product = lax.dot_general(
            mine, block, (((1,), (1,)), ((), ())), preferred_element_type=jnp.float32
        )
        bend = jnp.tanh(half * product + shift)
        equal = jnp.concatenate([columns[side]] * (block.shape[0] // 128), axis=1) == row
        coef = half * bend + jnp.where(equal, -half, half)
        return coef.astype(jnp.bfloat16), 1.0 - jnp.where(equal, -bend, bend)

    def unit(side, block, row, first=False):
        total_ref = (image_grad_ref, text_grad_ref)[side]
        coef, kept = weigh(side, block, row)
        if side == TEXT:
            wide = kept[:, :128]
            for group in range(1, block.shape[0] // 128):
                wide = wide * kept[:, group * 128 : (group + 1) * 128]
            loss_ref[...] += jnp.log(wide)
        part = jnp.dot(coef, block, preferred_element_type=jnp.float32)
        if first:
            total_ref[...] = part
        else:
            total_ref[...] += part

    def slot_tags(side, piece, slots):
        span = pl.ds(pl.multiple_of(piece * ROWS, ROWS), ROWS)
        return jnp.concatenate([tags[slot, side : side + 1, span] for slot in slots], axis=1)

    def slot_unit(side, piece, low, high):
        block = held[side, piece, low : high + 1].reshape(-1, held.shape[-1])
        unit(side, block, slot_tags(side, piece, range(low, high + 1)))

    for side in (TEXT, IMAGE):
        block = own[side].reshape(-1, own.shape[-1])
        unit(side, block, own_tags[side : side + 1, :], first=True)

    send_tags(IN1).wait_recv()

    def near_body(piece, carry):
        for side in (TEXT, IMAGE):
            send(IN1, side, piece).wait_recv()
        for side in (TEXT, IMAGE):
            slot_unit(side, piece, IN1, IN1)
        return carry

    lax.fori_loop(0, pieces, near_body, 0)

    send_tags(OUT1).wait_recv()
    send_tags(IN2).start()
    send_tags(OUT3).start()
    send_tags(IN3).wait_recv()
    send_tags(OUT2).start()
    send_tags(IN2).wait_recv()
    send_tags(OUT2).wait_recv()
    send_tags(OUT3).wait_recv()

    def relayed(side, piece):
        send(OUT3, side, piece).wait_recv()
        slot_unit(side, piece, OUT3, OUT3)

    def pass_on(side, piece):
        send(OUT1, side, piece).wait_recv()
        send(OUT3, side, piece).start()
        send(IN2, side, piece).start()

        @pl.when(piece + LEAD < pieces)
        def _():
            send(IN3, side, piece + LEAD).start()

        if side == TEXT:

            @pl.when(piece + LEAD >= pieces)
            def _():
                send(IN3, IMAGE, piece + LEAD - pieces).start()

    def work(side, piece):
        send(IN3, side, piece).wait_recv()
        send(OUT2, side, piece).start()
        slot_unit(side, piece, OUT1, IN3)
        send(IN2, side, piece).wait_recv()
        send(OUT2, side, piece).wait_recv()
        slot_unit(side, piece, IN2, OUT2)

    for side in (TEXT, IMAGE):

        def body(piece, carry, side=side):
            pass_on(side, piece)

            @pl.when(piece > 0)
            def _():
                work(side, piece - 1)

            @pl.when(piece > 1)
            def _():
                relayed(side, piece - 2)

            if side == IMAGE:

                @pl.when(piece == 0)
                def _():
                    work(TEXT, pieces - 1)
                    relayed(TEXT, pieces - 2)

                @pl.when(piece == 1)
                def _():
                    relayed(TEXT, pieces - 1)

            return carry

        lax.fori_loop(0, pieces, body, 0)

    work(IMAGE, pieces - 1)
    relayed(IMAGE, pieces - 2)

    send(OUT3, IMAGE, pieces - 1).wait_recv()
    block = held[IMAGE, pieces - 1, OUT3]
    coef_ref[...] = weigh(IMAGE, block, slot_tags(IMAGE, pieces - 1, [OUT3]))[0]
    block_ref[...] = block

    for slot in range(6):
        send_tags(slot).wait_send()

        def drain(piece, carry, slot=slot):
            for side in (TEXT, IMAGE):
                send(slot, side, piece).wait_send()
            return carry

        lax.fori_loop(0, pieces, drain, 0)


def finish(
    loss_ref, image_grad_ref, text_grad_ref, coef_ref, block_ref, loss_out, image_out, text_out, total, sem
):
    rows, lanes = loss_ref.shape
    copies = []

    def write(side, piece):
        span = pl.ds(piece * ROWS, ROWS)
        source, target = ((total, text_out), (image_grad_ref, image_out))[side]
        copy = pltpu.make_async_copy(source.at[span], target.at[span], sem.at[side, piece])
        copy.start()
        copies.append(copy)

    for piece in range(rows // ROWS):
        write(IMAGE, piece)
    for piece in range(rows // ROWS):
        span = pl.ds(piece * ROWS, ROWS)
        total[span] = text_grad_ref[span] + jnp.dot(
            coef_ref[span], block_ref[...], preferred_element_type=jnp.float32
        )
        write(TEXT, piece)
    sums = lax.dot_general(
        jnp.ones((8, lanes), jnp.float32),
        loss_ref[...],
        (((1,), (1,)), ((), ())),
        precision=lax.Precision.HIGHEST,
        preferred_element_type=jnp.float32,
    )
    loss = math.log(2.0) - sums[0:1] / ((2 * REACH + 1) * rows)
    loss_out[...] = loss.reshape(rows)
    for copy in copies:
        copy.wait()


def shards(
    picture_vectors,
    caption_vectors,
    photo_couple_tags,
    caption_match_ids,
    affinity_stretch,
    score_offset,
):
    rows, width = picture_vectors.shape
    pieces = rows // ROWS
    operands = (
        affinity_stretch,
        score_offset,
        picture_vectors,
        caption_vectors,
        photo_couple_tags,
        caption_match_ids,
    )
    vmem = pl.BlockSpec(memory_space=pltpu.VMEM)
    hbm = pl.BlockSpec(memory_space=pltpu.HBM)
    parts = pl.pallas_call(
        kernel,
        out_shape=(
            pltpu.VMEM((rows, 128), jnp.float32),
            pltpu.VMEM((rows, width), jnp.float32),
            pltpu.VMEM((rows, width), jnp.float32),
            pltpu.VMEM((rows, ROWS), jnp.bfloat16),
            pltpu.VMEM((ROWS, width), jnp.bfloat16),
        ),
        in_specs=[hbm] * 6,
        out_specs=(vmem,) * 5,
        scratch_shapes=[
            pltpu.VMEM((2, pieces, ROWS, width), jnp.bfloat16),
            pltpu.VMEM((2, pieces, ROWS, width), jnp.bfloat16),
            pltpu.VMEM((2, pieces, 6, ROWS, width), jnp.bfloat16),
            pltpu.SMEM((1,), jnp.float32),
            pltpu.SMEM((1,), jnp.float32),
            [pltpu.VMEM((rows,), jnp.int32)] * 2,
            pltpu.VMEM((8, rows), jnp.int32),
            pltpu.VMEM((6, 8, rows), jnp.int32),
            pltpu.VMEM((2, rows, 128), jnp.int32),
            pltpu.SemaphoreType.DMA((2, pieces)),
            pltpu.SemaphoreType.DMA((4,)),
            pltpu.SemaphoreType.DMA((6, 2, pieces)),
            pltpu.SemaphoreType.DMA((6, 2, pieces)),
            pltpu.SemaphoreType.DMA((6,)),
            pltpu.SemaphoreType.DMA((6,)),
        ],
        compiler_params=pltpu.CompilerParams(
            collective_id=0, has_side_effects=True, vmem_limit_bytes=40 * 1024 * 1024
        ),
        name="window_loss",
    )(
        *(
            pltpu.with_memory_space_constraint(array, pltpu.HBM) if array.size > 1 else array
            for array in operands
        )
    )
    return pl.pallas_call(
        finish,
        out_shape=(
            jax.ShapeDtypeStruct((rows,), jnp.float32),
            jax.ShapeDtypeStruct((rows, width), jnp.float32),
            jax.ShapeDtypeStruct((rows, width), jnp.float32),
        ),
        in_specs=[vmem] * 5,
        out_specs=(vmem, hbm, hbm),
        scratch_shapes=[pltpu.VMEM((rows, width), jnp.float32), pltpu.SemaphoreType.DMA((2, pieces))],
        compiler_params=pltpu.CompilerParams(vmem_limit_bytes=8 * 1024 * 1024),
        name="write_out",
    )(*parts)


def solution(mesh):
    placed = (P("dp", None), P("dp", None), P("dp"), P("dp"), P(), P())
    return jax.shard_map(
        shards,
        mesh=mesh,
        in_specs=placed,
        out_specs=(P("dp"), P("dp", None), P("dp", None)),
        check_vma=False,
    )
```

```python
import math

import jax
import jax.numpy as jnp
from jax import lax
from jax.experimental import pallas as pl
from jax.experimental.pallas import tpu as pltpu
from jax.sharding import PartitionSpec as P

MESH = pl.DeviceIdType.MESH
REACH = 3
ROWS = 128
LEAD = 2
OUT1, IN3, IN2, OUT2, IN1, OUT3 = range(6)
TEXT, IMAGE = 0, 1


def kernel(
    stretch_hbm,
    offset_hbm,
    picture_ref,
    caption_ref,
    couple_ref,
    match_ref,
    loss_ref,
    image_grad_ref,
    text_grad_ref,
    coef_ref,
    block_ref,
    raw,
    own,
    held,
    stretch_ref,
    offset_ref,
    flat_tags,
    own_tags,
    tags,
    columns,
    load_sem,
    tag_load_sem,
    send_sem,
    recv_sem,
    tag_send_sem,
    tag_recv_sem,
):
    count = lax.axis_size("dp")
    me = lax.axis_index("dp")
    sign = 2 * lax.rem(me, 2) - 1
    pieces = own.shape[1]

    def at(steps):
        return lax.rem(me + steps * sign + count, count)

    target = {OUT1: at(1), IN3: at(-3), IN2: at(-1), OUT2: at(-1), IN1: at(-1), OUT3: at(-2)}

    barrier = pltpu.get_barrier_semaphore()
    for steps in (1, -3, -1, 2):
        pl.semaphore_signal(barrier, inc=1, device_id=(at(steps),), device_id_type=MESH)

    def load(side, piece):
        source = (caption_ref, picture_ref)[side]
        return pltpu.make_async_copy(
            source.at[pl.ds(piece * ROWS, ROWS)], raw.at[side, piece], load_sem.at[side, piece]
        )

    def load_tags(side):
        source = (match_ref, couple_ref)[side]
        return pltpu.make_async_copy(source, flat_tags[side], tag_load_sem.at[side])

    for side in (TEXT, IMAGE):
        load_tags(side).start()
    for side in (TEXT, IMAGE):
        for piece in range(pieces):
            load(side, piece).start()
    scalars = (
        pltpu.make_async_copy(stretch_hbm, stretch_ref, tag_load_sem.at[2]),
        pltpu.make_async_copy(offset_hbm, offset_ref, tag_load_sem.at[3]),
    )
    for copy in scalars:
        copy.start()

    def normalize(side, piece):
        load(side, piece).wait()
        value = raw[side, piece].astype(jnp.float32)
        gain = lax.rsqrt(jnp.sum(value * value, axis=-1, keepdims=True) + 1e-06)
        own[side, piece] = (value * gain).astype(jnp.bfloat16)

    def source_of(slot, side, piece):
        if slot in (OUT1, IN3, IN1):
            return own.at[side, piece]
        return held.at[side, piece, IN3 if slot == OUT2 else OUT1]

    def send(slot, side, piece):
        return pltpu.make_async_remote_copy(
            src_ref=source_of(slot, side, piece),
            dst_ref=held.at[side, piece, slot],
            send_sem=send_sem.at[slot, side, piece],
            recv_sem=recv_sem.at[slot, side, piece],
            device_id=(target[slot],),
            device_id_type=MESH,
        )

    def send_tags(slot):
        if slot in (OUT1, IN3, IN1):
            source = own_tags
        else:
            source = tags.at[IN3 if slot == OUT2 else OUT1]
        return pltpu.make_async_remote_copy(
            src_ref=source,
            dst_ref=tags.at[slot],
            send_sem=tag_send_sem.at[slot],
            recv_sem=tag_recv_sem.at[slot],
            device_id=(target[slot],),
            device_id_type=MESH,
        )

    rows = own_tags.shape[1]
    for side in (TEXT, IMAGE):
        load_tags(side).wait()
        own_tags[side : side + 1, :] = flat_tags[side][...].reshape(1, rows)
    own_tags[2:8, :] = jnp.zeros((6, own_tags.shape[1]), jnp.int32)
    normalize(TEXT, 0)
    pl.semaphore_wait(barrier, 4)
    for slot in (OUT1, IN3, IN1):
        send_tags(slot).start()
    for side in (TEXT, IMAGE):
        for piece in range(pieces):
            if piece or side:
                normalize(side, piece)
            send(OUT1, side, piece).start()
            if side == TEXT and piece < LEAD:
                send(IN3, side, piece).start()
    for side in (TEXT, IMAGE):
        for piece in range(pieces):
            send(IN1, side, piece).start()

    for side in (TEXT, IMAGE):
        for piece in range(pieces):
            row = own_tags[1 - side : 2 - side, piece * ROWS : (piece + 1) * ROWS]
            columns[side, piece * ROWS : (piece + 1) * ROWS, :] = jnp.broadcast_to(
                row, (128, ROWS)
            ).T

    for copy in scalars:
        copy.wait()
    half = 0.5 * stretch_ref[0]
    shift = 0.5 * offset_ref[0]
    loss_ref[...] = jnp.zeros_like(loss_ref)

    def weigh(side, block, row):
        mine = own[1 - side].reshape(-1, block.shape[1])
        product = lax.dot_general(
            mine, block, (((1,), (1,)), ((), ())), preferred_element_type=jnp.float32
        )
        bend = jnp.tanh(half * product + shift)
        equal = jnp.concatenate([columns[side]] * (block.shape[0] // 128), axis=1) == row
        coef = half * bend + jnp.where(equal, -half, half)
        return coef.astype(jnp.bfloat16), 1.0 - jnp.where(equal, -bend, bend)

    def unit(side, block, row, first=False):
        total_ref = (image_grad_ref, text_grad_ref)[side]
        coef, kept = weigh(side, block, row)
        if side == TEXT:
            wide = kept[:, :128]
            for group in range(1, block.shape[0] // 128):
                wide = wide * kept[:, group * 128 : (group + 1) * 128]
            loss_ref[...] += jnp.log(wide)
        part = jnp.dot(coef, block, preferred_element_type=jnp.float32)
        if first:
            total_ref[...] = part
        else:
            total_ref[...] += part

    def slot_tags(side, piece, slots):
        span = pl.ds(pl.multiple_of(piece * ROWS, ROWS), ROWS)
        return jnp.concatenate([tags[slot, side : side + 1, span] for slot in slots], axis=1)

    def slot_unit(side, piece, low, high):
        block = held[side, piece, low : high + 1].reshape(-1, held.shape[-1])
        unit(side, block, slot_tags(side, piece, range(low, high + 1)))

    for side in (TEXT, IMAGE):
        block = own[side].reshape(-1, own.shape[-1])
        unit(side, block, own_tags[side : side + 1, :], first=True)

    send_tags(IN1).wait_recv()

    def near_body(piece, carry):
        for side in (TEXT, IMAGE):
            send(IN1, side, piece).wait_recv()
        for side in (TEXT, IMAGE):
            slot_unit(side, piece, IN1, IN1)
        return carry

    lax.fori_loop(0, pieces, near_body, 0)

    send_tags(OUT1).wait_recv()
    send_tags(IN2).start()
    send_tags(OUT3).start()
    send_tags(IN3).wait_recv()
    send_tags(OUT2).start()
    send_tags(IN2).wait_recv()
    send_tags(OUT2).wait_recv()
    send_tags(OUT3).wait_recv()

    def relayed(side, piece):
        send(OUT3, side, piece).wait_recv()
        slot_unit(side, piece, OUT3, OUT3)

    def pass_on(side, piece):
        send(OUT1, side, piece).wait_recv()
        send(OUT3, side, piece).start()
        send(IN2, side, piece).start()

        @pl.when(piece + LEAD < pieces)
        def _():
            send(IN3, side, piece + LEAD).start()

        if side == TEXT:

            @pl.when(piece + LEAD >= pieces)
            def _():
                send(IN3, IMAGE, piece + LEAD - pieces).start()

    def work(side, piece):
        send(IN3, side, piece).wait_recv()
        send(OUT2, side, piece).start()
        slot_unit(side, piece, OUT1, IN3)
        send(IN2, side, piece).wait_recv()
        send(OUT2, side, piece).wait_recv()
        slot_unit(side, piece, IN2, OUT2)

    for side in (TEXT, IMAGE):

        def body(piece, carry, side=side):
            pass_on(side, piece)

            @pl.when(piece > 0)
            def _():
                work(side, piece - 1)

            @pl.when(piece > 1)
            def _():
                relayed(side, piece - 2)

            if side == IMAGE:

                @pl.when(piece == 0)
                def _():
                    work(TEXT, pieces - 1)
                    relayed(TEXT, pieces - 2)

                @pl.when(piece == 1)
                def _():
                    relayed(TEXT, pieces - 1)

            return carry

        lax.fori_loop(0, pieces, body, 0)

    work(IMAGE, pieces - 1)
    relayed(IMAGE, pieces - 2)

    send(OUT3, IMAGE, pieces - 1).wait_recv()
    block = held[IMAGE, pieces - 1, OUT3]
    coef_ref[...] = weigh(IMAGE, block, slot_tags(IMAGE, pieces - 1, [OUT3]))[0]
    block_ref[...] = block

    for slot in range(6):
        send_tags(slot).wait_send()

        def drain(piece, carry, slot=slot):
            for side in (TEXT, IMAGE):
                send(slot, side, piece).wait_send()
            return carry

        lax.fori_loop(0, pieces, drain, 0)


def finish(
    loss_ref, image_grad_ref, text_grad_ref, coef_ref, block_ref, loss_out, image_out, text_out, total, sem
):
    rows, lanes = loss_ref.shape
    copies = []

    def write(side, piece):
        span = pl.ds(piece * ROWS, ROWS)
        source, target = ((total, text_out), (image_grad_ref, image_out))[side]
        copy = pltpu.make_async_copy(source.at[span], target.at[span], sem.at[side, piece])
        copy.start()
        copies.append(copy)

    for piece in range(rows // ROWS):
        write(IMAGE, piece)
    for piece in range(rows // ROWS):
        span = pl.ds(piece * ROWS, ROWS)
        total[span] = text_grad_ref[span] + jnp.dot(
            coef_ref[span], block_ref[...], preferred_element_type=jnp.float32
        )
        write(TEXT, piece)
    sums = lax.dot_general(
        jnp.ones((8, lanes), jnp.float32),
        loss_ref[...],
        (((1,), (1,)), ((), ())),
        precision=lax.Precision.HIGHEST,
        preferred_element_type=jnp.float32,
    )
    loss = math.log(2.0) - sums[0:1] / ((2 * REACH + 1) * rows)
    loss_out[...] = loss.reshape(rows)
    for copy in copies:
        copy.wait()


def shards(
    picture_vectors,
    caption_vectors,
    photo_couple_tags,
    caption_match_ids,
    affinity_stretch,
    score_offset,
):
    rows, width = picture_vectors.shape
    pieces = rows // ROWS
    operands = (
        affinity_stretch,
        score_offset,
        picture_vectors,
        caption_vectors,
        photo_couple_tags,
        caption_match_ids,
    )
    vmem = pl.BlockSpec(memory_space=pltpu.VMEM)
    hbm = pl.BlockSpec(memory_space=pltpu.HBM)
    parts = pl.pallas_call(
        kernel,
        out_shape=(
            pltpu.VMEM((rows, 128), jnp.float32),
            pltpu.VMEM((rows, width), jnp.float32),
            pltpu.VMEM((rows, width), jnp.float32),
            pltpu.VMEM((rows, ROWS), jnp.bfloat16),
            pltpu.VMEM((ROWS, width), jnp.bfloat16),
        ),
        in_specs=[hbm] * 6,
        out_specs=(vmem,) * 5,
        scratch_shapes=[
            pltpu.VMEM((2, pieces, ROWS, width), jnp.bfloat16),
            pltpu.VMEM((2, pieces, ROWS, width), jnp.bfloat16),
            pltpu.VMEM((2, pieces, 6, ROWS, width), jnp.bfloat16),
            pltpu.SMEM((1,), jnp.float32),
            pltpu.SMEM((1,), jnp.float32),
            [pltpu.VMEM((rows,), jnp.int32)] * 2,
            pltpu.VMEM((8, rows), jnp.int32),
            pltpu.VMEM((6, 8, rows), jnp.int32),
            pltpu.VMEM((2, rows, 128), jnp.int32),
            pltpu.SemaphoreType.DMA((2, pieces)),
            pltpu.SemaphoreType.DMA((4,)),
            pltpu.SemaphoreType.DMA((6, 2, pieces)),
            pltpu.SemaphoreType.DMA((6, 2, pieces)),
            pltpu.SemaphoreType.DMA((6,)),
            pltpu.SemaphoreType.DMA((6,)),
        ],
        compiler_params=pltpu.CompilerParams(
            collective_id=0, has_side_effects=True, vmem_limit_bytes=40 * 1024 * 1024
        ),
        name="window_loss",
    )(
        *(
            pltpu.with_memory_space_constraint(array, pltpu.HBM) if array.size > 1 else array
            for array in operands
        )
    )
    return pl.pallas_call(
        finish,
        out_shape=(
            jax.ShapeDtypeStruct((rows,), jnp.float32),
            jax.ShapeDtypeStruct((rows, width), jnp.float32),
            jax.ShapeDtypeStruct((rows, width), jnp.float32),
        ),
        in_specs=[vmem] * 5,
        out_specs=(vmem, hbm, hbm),
        scratch_shapes=[pltpu.VMEM((rows, width), jnp.float32), pltpu.SemaphoreType.DMA((2, pieces))],
        compiler_params=pltpu.CompilerParams(vmem_limit_bytes=8 * 1024 * 1024),
        name="write_out",
    )(*parts)


def solution(mesh):
    placed = (P("dp", None), P("dp", None), P("dp"), P("dp"), P(), P())
    return jax.shard_map(
        shards,
        mesh=mesh,
        in_specs=placed,
        out_specs=(P("dp"), P("dp", None), P("dp", None)),
        check_vma=False,
    )
```
